32 devices in a mesh: dp: 8 (over y, x, core), tensor: 4 (over z).
Axes of the slice: x: 2, y: 2, z: 4, core: 2. Of those that a mesh axis runs over, the one named last changes fastest.
Arguments:
- tokens: bfloat16 [8192, 1024], P(('dp', 'tensor')), may hold values from -6 to 6
- cotangent: bfloat16 [8192, 1024], P(('dp', 'tensor')), may hold values from -6 to 6
- norm_gain: float32 [1024], replicated, may hold values from 0.1 to 1.9
- w_gate: bfloat16 [1024, 2048], P('dp', 'tensor'), may hold values from -0.1875 to 0.1875
- w_value: bfloat16 [1024, 2048], P('dp', 'tensor'), may hold values from -0.1875 to 0.1875
- w_bc: bfloat16 [1024, 256], P('dp'), may hold values from -0.1875 to 0.1875
- w_step: bfloat16 [1024, 32], P('dp', 'tensor'), may hold values from -0.1875 to 0.1875
- conv_value: float32 [5, 2048], P(None, 'tensor'), may hold values from -3 to 3
- conv_bc: float32 [5, 256], replicated, may hold values from -3 to 3
- head_params: float32 [3, 32], P(None, 'tensor'), may hold values from -2 to 1
- gnorm_gain: float32 [2048], P('tensor'), may hold values from 0.1 to 1.9
- w_out: bfloat16 [2048, 1024], P('tensor', 'dp'), may hold values from -0.125 to 0.125
Outputs:
- block_out: float32 [8192, 1024], P(('dp', 'tensor'))
- grad_input: float32 [8192, 1024], P(('dp', 'tensor'))
- grad_norm_gain: float32 [1024], replicated
- grad_w_gate: float32 [1024, 2048], P('dp', 'tensor')
- grad_w_value: float32 [1024, 2048], P('dp', 'tensor')
- grad_w_bc: float32 [1024, 256], P('dp')
- grad_w_step: float32 [1024, 32], P('dp', 'tensor')
- grad_conv_value: float32 [5, 2048], P(None, 'tensor')
- grad_conv_bc: float32 [5, 256], replicated
- grad_head_params: float32 [3, 32], P(None, 'tensor')
- grad_gnorm_gain: float32 [2048], P('tensor')
- grad_w_out: float32 [2048, 1024], P('tensor', 'dp')
The draws below stay inside these ranges and needn't reach their ends.
All inputs are finite; a program needn't handle non-finite values.
Results may differ from the reference program's by a relative error of at most 0.02.
Values may be sent and summed in bfloat16 or wider, within the bound.
A program may use at most 128 MiB of HBM per device.

```python
import jax
import jax.numpy as jnp
from jax import lax

D = 1024
HEADS = 32
STATE = 128
CONVW = 4
SPAN = 256
SEQLEN = 1024
INNER = 2048
TOKENS = 8192


def steps_of(key, extent, cuts, smallest, top_value):
    loudness, own = 1.0, jax.random.fold_in(key, 6)
    for position, parts in cuts:
        draws = jnp.exp(jax.random.uniform(jax.random.fold_in(own, position), (parts,), jnp.float32, smallest / len(cuts), top_value / len(cuts)))
        loudness = loudness * jnp.repeat(draws, extent[position] // parts).reshape([-1 if axis == position else 1 for axis in range(len(extent))])
    return loudness


def centred(own_key, shape, scale, most, pieces=(), dtype=jnp.bfloat16):
    loudness = steps_of(own_key, shape, pieces, -0.22, 0.18) if pieces else 1.0
    drawn = jax.random.normal(own_key, shape, jnp.float32) * scale * loudness
    return jnp.minimum(jnp.maximum(drawn, -most), most).astype(dtype)


def setup_inputs(seed: int = 0) -> dict:
    key_of = jax.random.split(jax.random.key(seed), 13)
    tokens = centred(key_of[0], (TOKENS, D), 1.0, 6.0, ((0, 32),))
    cotangent = centred(key_of[1], (TOKENS, D), 1.0, 6.0, ((0, 32),))
    norm_gain = jnp.clip(1.0 + 0.18 * jax.random.normal(key_of[2], (D,), jnp.float32), 0.1, 1.9)
    w_gate = centred(key_of[3], (D, INNER), D ** -0.5, 0.1875, ((0, 8), (1, 4)))
    w_value = centred(key_of[4], (D, INNER), D ** -0.5, 0.1875, ((0, 8), (1, 4)))
    w_bc = centred(key_of[5], (D, 2 * STATE), D ** -0.5, 0.1875, ((0, 8),))
    w_step = centred(key_of[6], (D, HEADS), D ** -0.5, 0.1875, ((0, 8), (1, 4)))
    conv_value = centred(key_of[7], (CONVW + 1, INNER), 0.5, 3.0, ((1, 4),), jnp.float32)
    conv_bc = centred(key_of[8], (CONVW + 1, 2 * STATE), 0.5, 3.0, (), jnp.float32)
    head_params = jnp.clip(-2.0 + 3.0 * jax.random.uniform(key_of[9], (3, HEADS), jnp.float32) ** steps_of(key_of[9], (3, HEADS), ((1, 4),), -0.2, 0.2), -2.0, 1.0)
    gnorm_gain = jnp.clip(1.0 + 0.18 * jax.random.normal(key_of[10], (INNER,), jnp.float32), 0.1, 1.9)
    w_out = centred(key_of[11], (INNER, D), INNER ** -0.5, 0.125, ((0, 4), (1, 8)))
    return {"tokens": tokens, "cotangent": cotangent, "norm_gain": norm_gain, "w_gate": w_gate, "w_value": w_value, "w_bc": w_bc, "w_step": w_step, "conv_value": conv_value, "conv_bc": conv_bc, "head_params": head_params, "gnorm_gain": gnorm_gain, "w_out": w_out}


EPSILON = 1e-05
HIGHEST = lax.Precision.HIGHEST

@jax.custom_vjp
def low(v):
    return lax.optimization_barrier(v.astype(jnp.bfloat16)).astype(jnp.float32)

@jax.custom_vjp
def low_back(v):
    return v

def low_keep(v):
    return (low(v), None)

def low_pass(kept, grad):
    return (grad,)

def back_keep(v):
    return (v, None)

def back_low(kept, grad):
    return (low(grad),)
low.defvjp(low_keep, low_pass)
low_back.defvjp(back_keep, back_low)

def causal(sequence, taps):
    width = taps.shape[0] - 1
    padded = jnp.pad(sequence, ((width - 1, 0), (0, 0)))
    total = jnp.zeros_like(sequence) + taps[width]
    for offset in range(width):
        total = total + taps[offset] * padded[offset:offset + sequence.shape[0]]
    return total

def scan_state(values, step_size, rate, b_map, c_map):
    length, heads, hdim_local = values.shape
    count = length // SPAN
    values_c = values.reshape(count, SPAN, heads, hdim_local)
    step_c = step_size.reshape(count, SPAN, heads)
    b_c = b_map.reshape(count, SPAN, b_map.shape[1])
    c_c = c_map.reshape(count, SPAN, c_map.shape[1])
    lower = (lax.broadcasted_iota(jnp.int32, (SPAN, SPAN), 0) >= lax.broadcasted_iota(jnp.int32, (SPAN, SPAN), 1))[None, :, :]

    def span_step(state, block):
        block_values, block_step, block_b, block_c = block
        logdecay = jnp.cumsum(block_step * rate[None, :], axis=0)
        heads_first = logdecay.T
        inner_prod = jnp.dot(block_c, block_b.T, precision=HIGHEST, preferred_element_type=jnp.float32)
        spacing = heads_first[:, :, None] - heads_first[:, None, :]
        kernel = jnp.where(lower, jnp.exp(jnp.where(lower, spacing, -60.0)), 0.0)
        kernel = kernel * inner_prod[None, :, :] * block_step.T[:, None, :]
        within = jnp.einsum('hij,jhp->ihp', kernel, block_values, precision=HIGHEST)
        carried = jnp.einsum('in,hpn->ihp', block_c, state, precision=HIGHEST) * jnp.exp(logdecay)[:, :, None]
        trailing = jnp.exp(logdecay[-1][None, :] - logdecay) * block_step
        update = jnp.einsum('jh,jhp,jn->hpn', trailing, block_values, block_b, precision=HIGHEST)
        new_state = state * jnp.exp(logdecay[-1])[:, None, None] + update
        return (new_state, within + carried)
    start = jnp.zeros((heads, hdim_local, b_map.shape[1]), jnp.float32)
    final_state, outputs = lax.scan(jax.checkpoint(span_step), start, (values_c, step_c, b_c, c_c))
    return outputs.reshape(length, heads, hdim_local)

def mixer(gate_pre, value_pre, shared_pre, step_pre, conv_value, conv_bc, head_params):
    length = gate_pre.shape[0]
    heads = step_pre.shape[1]
    values = jax.nn.silu(causal(value_pre, conv_value))
    shared = jax.nn.silu(causal(shared_pre, conv_bc))
    half_width = shared.shape[1] // 2
    step_size = jax.nn.softplus(step_pre + head_params[0])
    rate = -jnp.exp(head_params[1])
    headed = values.reshape(length, heads, -1)
    scanned = scan_state(headed, step_size, rate, shared[:, :half_width], shared[:, half_width:])
    scanned = scanned + head_params[2][None, :, None] * headed
    return scanned.reshape(length, -1) * jax.nn.silu(gate_pre)

def mat(left, right):
    return jnp.dot(left, right, precision=HIGHEST, preferred_element_type=jnp.float32)

def layer(rows, norm_gain, w_gate, w_value, w_bc, w_step, conv_value, conv_bc, head_params, gnorm_gain, w_out):
    scaling = lax.rsqrt(lax.optimization_barrier(jnp.mean(rows * rows, axis=1, keepdims=True)) + EPSILON)
    normed = low(rows * scaling * norm_gain)
    gate_pre = low_back(mat(normed, w_gate))
    value_pre = low_back(mat(normed, w_value))
    shared_pre = low_back(mat(normed, w_bc))
    step_pre = low_back(mat(normed, w_step))
    gated = mixer(gate_pre, value_pre, shared_pre, step_pre, conv_value, conv_bc, head_params)
    rescale = lax.rsqrt(lax.optimization_barrier(jnp.mean(gated * gated, axis=1, keepdims=True)) + EPSILON)
    scaled = low(gated * rescale * gnorm_gain)
    return rows + low_back(mat(scaled, w_out))

def reference(tokens, cotangent, norm_gain, w_gate, w_value, w_bc, w_step, conv_value, conv_bc, head_params, gnorm_gain, w_out):
    floats = [array.astype(jnp.float32) for array in (tokens, norm_gain, w_gate, w_value, w_bc, w_step, conv_value, conv_bc, head_params, gnorm_gain, w_out)]

    def forward(rows, *weights):
        blocks = rows.reshape(-1, SEQLEN, rows.shape[1])

        def one_sequence(block):
            return layer(block, *weights)
        outputs = lax.map(jax.checkpoint(one_sequence), blocks)
        return outputs.reshape(rows.shape)
    block_out, pullback = jax.vjp(forward, *floats)
    grads = pullback(cotangent.astype(jnp.float32))
    return (block_out, grads[0], grads[1], grads[2], grads[3], grads[4], grads[5], grads[6], grads[7], grads[8], grads[9], grads[10])
```

```python
import functools

import jax
import jax.numpy as jnp
from jax import lax
from jax.experimental import pallas as pl
from jax.experimental.pallas import tpu as pltpu
from jax.sharding import PartitionSpec as P

D = 1024
SPAN = 256
SEQLEN = 1024
INNER = 2048
LANES = 128

EPSILON = 1e-05
HIGHEST = lax.Precision.HIGHEST
MESH = pl.DeviceIdType.MESH


def causal(sequence, taps):
    width = taps.shape[0] - 1
    padded = jnp.pad(sequence, ((width - 1, 0), (0, 0)))
    total = jnp.zeros_like(sequence) + taps[width]
    for offset in range(width):
        total = total + taps[offset] * padded[offset : offset + sequence.shape[0]]
    return total


def scan_state(values, step_size, rate, b_map, c_map):
    length, heads, hdim_local = values.shape
    count = length // SPAN
    values_c = values.reshape(count, SPAN, heads, hdim_local)
    step_c = step_size.reshape(count, SPAN, heads)
    b_c = b_map.reshape(count, SPAN, b_map.shape[1])
    c_c = c_map.reshape(count, SPAN, c_map.shape[1])
    lower = (
        lax.broadcasted_iota(jnp.int32, (SPAN, SPAN), 0)
        >= lax.broadcasted_iota(jnp.int32, (SPAN, SPAN), 1)
    )[None, :, :]

    def span_step(state, block):
        block_values, block_step, block_b, block_c = block
        logdecay = jnp.cumsum(block_step * rate[None, :], axis=0)
        heads_first = logdecay.T
        inner_prod = jnp.dot(
            block_c, block_b.T, precision=HIGHEST, preferred_element_type=jnp.float32
        )
        spacing = heads_first[:, :, None] - heads_first[:, None, :]
        kernel = jnp.where(lower, jnp.exp(jnp.where(lower, spacing, -60.0)), 0.0)
        kernel = kernel * inner_prod[None, :, :] * block_step.T[:, None, :]
        within = jnp.einsum("hij,jhp->ihp", kernel, block_values, precision=HIGHEST)
        carried = (
            jnp.einsum("in,hpn->ihp", block_c, state, precision=HIGHEST)
            * jnp.exp(logdecay)[:, :, None]
        )
        trailing = jnp.exp(logdecay[-1][None, :] - logdecay) * block_step
        update = jnp.einsum("jh,jhp,jn->hpn", trailing, block_values, block_b, precision=HIGHEST)
        new_state = state * jnp.exp(logdecay[-1])[:, None, None] + update
        return (new_state, within + carried)

    start = jnp.zeros((heads, hdim_local, b_map.shape[1]), jnp.float32)
    final_state, outputs = lax.scan(jax.checkpoint(span_step), start, (values_c, step_c, b_c, c_c))
    return outputs.reshape(length, heads, hdim_local)


def mixer(gate_pre, value_pre, shared_pre, step_pre, conv_value, conv_bc, head_params):
    length = gate_pre.shape[0]
    heads = step_pre.shape[1]
    values = jax.nn.silu(causal(value_pre, conv_value))
    shared = jax.nn.silu(causal(shared_pre, conv_bc))
    half_width = shared.shape[1] // 2
    step_size = jax.nn.softplus(step_pre + head_params[0])
    rate = -jnp.exp(head_params[1])
    headed = values.reshape(length, heads, -1)
    scanned = scan_state(headed, step_size, rate, shared[:, :half_width], shared[:, half_width:])
    scanned = scanned + head_params[2][None, :, None] * headed
    return scanned.reshape(length, -1) * jax.nn.silu(gate_pre)


def contract_rows(left, right):
    return lax.dot_general(
        left, right, (((0,), (0,)), ((), ())), preferred_element_type=jnp.float32
    )


def contract_cols(left, right):
    return lax.dot_general(
        left, right, (((1,), (1,)), ((), ())), preferred_element_type=jnp.float32
    )


def bits_of(size):
    found, bit = [], 1
    while bit < size:
        found.append(bit)
        bit *= 2
    return found


def flip(index, bit):
    return index + bit - 2 * bit * ((index // bit) % 2)


def flip_all(index, mask, bits):
    for bit in bits:
        if mask & bit:
            index = flip(index, bit)
    return index


def reduce_kernel(
    dp, tensor, bc_at, shared_rows, p_ref, small_ref, out_ref, small_out,
    acc, slots, small_slots, bc_send, bc_slots, tsmall_slots,
    send_sem, recv_sem, ssend, srecv, tsend, trecv,
):
    me, rank = lax.axis_index("dp"), lax.axis_index("tensor")
    bits, tbits = bits_of(dp), bits_of(tensor)
    width = p_ref.shape[2]
    cut = (width // LANES + 1) // 2 * LANES
    halves = ((0, cut), (cut, width - cut))
    orders = (bits, bits[:1] + bits[2:] + bits[1:2])
    count = small_ref.shape[0]
    barrier = pltpu.get_barrier_semaphore()
    for bit in bits:
        pl.semaphore_signal(barrier, inc=1, device_id=(flip(me, bit), rank), device_id_type=MESH)
    for bit in tbits:
        pl.semaphore_signal(barrier, inc=1, device_id=(me, flip(rank, bit)), device_id_type=MESH)
    pl.semaphore_wait(barrier, len(bits) + len(tbits))

    slot_of = {}
    sets = []
    for half in range(2):
        order = orders[half]
        seen, number, phases = 0, 0, []
        for phase, bit in enumerate(order):
            seen |= bit
            kept = [r for r in range(dp) if r & seen == 0]
            if phase + 1 < len(order):
                kept.sort(key=lambda r: -(r & order[phase + 1]))
            phases.append(kept)
            for r in kept:
                slot_of[half, phase, r] = number
                number += 1
        sets.append(phases)

    def copy_of(half, phase, r):
        bit = orders[half][phase]
        at, size = halves[half]
        columns = pl.ds(at, size)
        slot = slot_of[half, phase, r]
        if phase == 0:
            source = p_ref.at[flip_all(me, r | bit, bits), :, columns]
        else:
            source = acc.at[r | bit, :, columns]
        return pltpu.make_async_remote_copy(
            src_ref=source,
            dst_ref=slots.at[slot, :, columns],
            send_sem=send_sem.at[half, slot],
            recv_sem=recv_sem.at[half, slot],
            device_id=(flip(me, bit), rank),
            device_id_type=MESH,
        )

    small_out[...] = small_ref[...]
    copies = []

    def small_copy(phase):
        return pltpu.make_async_remote_copy(
            src_ref=small_out,
            dst_ref=small_slots.at[phase],
            send_sem=ssend.at[phase],
            recv_sem=srecv.at[phase],
            device_id=(flip(me, bits[phase]), rank),
            device_id_type=MESH,
        )

    for r_at in range(len(sets[0][0])):
        for half in range(2):
            copy = copy_of(half, 0, sets[half][0][r_at])
            copy.start()
            copies.append(copy)
    for phase in range(len(bits)):
        small = small_copy(phase)
        small.start()
        small.wait()
        small_out[...] += small_slots[phase]
        for r_at in range(len(sets[0][phase])):
            for half in range(2):
                order = orders[half]
                at, size = halves[half]
                columns = pl.ds(at, size)
                r = sets[half][phase][r_at]
                copy_of(half, phase, r).wait_recv()
                arrived = slots[slot_of[half, phase, r], :, columns].astype(jnp.float32)
                if phase == 0:
                    own = p_ref[flip_all(me, r, bits), :, columns]
                else:
                    own = acc[r, :, columns]
                total = own.astype(jnp.float32) + arrived
                if phase + 1 == len(bits):
                    out_ref[:, columns] = total
                else:
                    acc[r, :, columns] = total.astype(jnp.bfloat16)
                    if r & order[phase + 1]:
                        copy = copy_of(half, phase + 1, r ^ order[phase + 1])
                        copy.start()
                        copies.append(copy)
    bc_cols = pl.ds(bc_at, bc_send.shape[1])
    first = count - shared_rows
    for phase, bit in enumerate(tbits):
        bc_send[...] = out_ref[:, bc_cols].astype(jnp.bfloat16)
        pair = []
        for which, (source, target) in enumerate(
            (
                (bc_send, bc_slots.at[phase]),
                (small_out.at[pl.ds(first, shared_rows)], tsmall_slots.at[phase]),
            )
        ):
            copy = pltpu.make_async_remote_copy(
                src_ref=source,
                dst_ref=target,
                send_sem=tsend.at[phase, which],
                recv_sem=trecv.at[phase, which],
                device_id=(me, flip(rank, bit)),
                device_id_type=MESH,
            )
            copy.start()
            pair.append(copy)
        for copy in pair:
            copy.wait()
        out_ref[:, bc_cols] += bc_slots[phase].astype(jnp.float32)
        small_out[pl.ds(first, shared_rows), :] += tsmall_slots[phase]
    for copy in copies:
        copy.wait_send()


def reduce_all(dp, tensor, packed, small, bc_at, bc_width, shared_rows):
    rows, width = packed.shape
    block = rows // dp
    n, t = len(bits_of(dp)), len(bits_of(tensor))
    vmem = pl.BlockSpec(memory_space=pltpu.VMEM)
    return pl.pallas_call(
        functools.partial(reduce_kernel, dp, tensor, bc_at, shared_rows),
        out_shape=(
            jax.ShapeDtypeStruct((block, width), jnp.float32),
            jax.ShapeDtypeStruct(small.shape, jnp.float32),
        ),
        in_specs=[vmem, vmem],
        out_specs=(vmem, vmem),
        scratch_shapes=[
            pltpu.VMEM((dp, block, width), jnp.bfloat16),
            pltpu.VMEM((dp - 1, block, width), jnp.bfloat16),
            pltpu.VMEM((n,) + small.shape, jnp.float32),
            pltpu.VMEM((block, bc_width), jnp.bfloat16),
            pltpu.VMEM((t, block, bc_width), jnp.bfloat16),
            pltpu.VMEM((t, shared_rows, LANES), jnp.float32),
            pltpu.SemaphoreType.DMA((2, dp - 1)),
            pltpu.SemaphoreType.DMA((2, dp - 1)),
            pltpu.SemaphoreType.DMA((n,)),
            pltpu.SemaphoreType.DMA((n,)),
            pltpu.SemaphoreType.DMA((t, 2)),
            pltpu.SemaphoreType.DMA((t, 2)),
        ],
        compiler_params=pltpu.CompilerParams(
            collective_id=0, has_side_effects=True, vmem_limit_bytes=48 * 1024 * 1024
        ),
    )(packed.reshape(dp, block, width), small)


def as_rows(parts, rows):
    flat = jnp.concatenate([part.reshape(-1) for part in parts])
    return jnp.pad(flat, (0, rows * LANES - flat.shape[0])).reshape(rows, LANES)


def body(
    dp,
    tensor,
    tokens,
    cotangent,
    norm_gain,
    w_gate,
    w_value,
    w_bc,
    w_step,
    conv_value,
    conv_bc,
    head_params,
    gnorm_gain,
    w_out,
):
    width, bc_width, heads = w_gate.shape[1], w_bc.shape[1], w_step.shape[1]
    rows32 = tokens.astype(jnp.float32)
    grad_out = cotangent.astype(jnp.float32)
    scaling = lax.rsqrt(jnp.mean(rows32 * rows32, axis=1, keepdims=True) + EPSILON)
    normed = lax.all_gather(
        (rows32 * scaling * norm_gain).astype(jnp.bfloat16), "tensor", axis=0, tiled=True
    )
    shard = jnp.concatenate(
        [w_gate, w_value, w_bc, jnp.pad(w_step, ((0, 0), (0, LANES - heads))), w_out.T], axis=1
    )
    fetched = lax.all_gather(shard, "dp", axis=0, tiled=True)
    grad_rows = lax.all_gather(cotangent, "tensor", axis=0, tiled=True)
    at = 2 * width + bc_width + LANES
    w_cat, w_out_t = fetched[:, :at], fetched[:, at:]
    projected = jnp.dot(normed, w_cat, preferred_element_type=jnp.float32)
    pieces = (
        projected[:, :width],
        projected[:, width : 2 * width],
        projected[:, 2 * width : 2 * width + bc_width],
        projected[:, 2 * width + bc_width : 2 * width + bc_width + heads],
    )
    gated, mix_back = jax.vjp(mixer, *pieces, conv_value, conv_bc, head_params)
    grad_scaled = jnp.dot(grad_rows, w_out_t, preferred_element_type=jnp.float32)
    grad_unit = grad_scaled * gnorm_gain
    sums = lax.psum(
        jnp.stack([jnp.sum(gated * gated, axis=1), jnp.sum(grad_unit * gated, axis=1)]), "tensor"
    )
    rescale = lax.rsqrt(sums[0] / INNER + EPSILON)[:, None]
    unitized = gated * rescale
    scaled = (unitized * gnorm_gain).astype(jnp.bfloat16)
    branch = contract_cols(scaled, w_out_t)
    block_out = rows32 + lax.psum_scatter(
        branch.astype(jnp.bfloat16), "tensor", scatter_dimension=0, tiled=True
    ).astype(jnp.float32)
    grad_w_out_t = contract_rows(grad_rows, scaled)
    grad_gnorm = jnp.sum(grad_scaled * unitized, axis=0)
    grad_gated = (
        rescale * grad_unit - gated * (rescale * rescale * rescale) * sums[1][:, None] / INNER
    )
    mix_grads = mix_back(grad_gated)
    grad_cat = jnp.concatenate(
        [piece.astype(jnp.bfloat16) for piece in mix_grads[:3]]
        + [jnp.pad(mix_grads[3].astype(jnp.bfloat16), ((0, 0), (0, LANES - heads)))],
        axis=1,
    )
    grad_conv_value, grad_conv_bc, grad_head = mix_grads[4:]
    grad_normed = contract_cols(grad_cat, w_cat)
    grad_h = lax.psum_scatter(
        grad_normed.astype(jnp.bfloat16), "tensor", scatter_dimension=0, tiled=True
    ).astype(jnp.float32)
    scaled_grad = grad_h * norm_gain
    grad_input = (
        grad_out
        + scaling * scaled_grad
        - rows32
        * (scaling * scaling * scaling)
        * jnp.sum(scaled_grad * rows32, axis=1, keepdims=True)
        / D
    )
    grad_norm_local = jnp.sum(grad_h * rows32 * scaling, axis=0)
    weight_terms = jnp.concatenate([contract_rows(normed, grad_cat), grad_w_out_t], axis=1)
    own_parts = [grad_conv_value, grad_gnorm, jnp.pad(grad_head, ((0, 0), (0, LANES - heads)))]
    own_rows = -(-(sum(part.size for part in own_parts)) // (8 * LANES)) * 8
    shared_parts = [grad_conv_bc, grad_norm_local]
    shared_rows = -(-(sum(part.size for part in shared_parts)) // (8 * LANES)) * 8
    small = jnp.concatenate([as_rows(own_parts, own_rows), as_rows(shared_parts, shared_rows)])
    summed, small = reduce_all(
        dp, tensor, weight_terms.astype(jnp.bfloat16), small, 2 * width, bc_width, shared_rows
    )
    own, shared = small[:own_rows].reshape(-1), small[own_rows:].reshape(-1)
    n_conv, n_bc = grad_conv_value.size, grad_conv_bc.size
    return (
        block_out,
        grad_input,
        shared[n_bc : n_bc + norm_gain.shape[0]],
        summed[:, :width],
        summed[:, width : 2 * width],
        summed[:, 2 * width : 2 * width + bc_width],
        summed[:, 2 * width + bc_width : 2 * width + bc_width + heads],
        own[:n_conv].reshape(grad_conv_value.shape),
        shared[:n_bc].reshape(grad_conv_bc.shape),
        own[n_conv + width : n_conv + width + 3 * LANES].reshape(3, LANES)[:, :heads],
        own[n_conv : n_conv + width],
        summed[:, at:].T,
    )


def solution(mesh):
    in_specs = (
        P(("dp", "tensor"), None),
        P(("dp", "tensor"), None),
        P(),
        P("dp", "tensor"),
        P("dp", "tensor"),
        P("dp", None),
        P("dp", "tensor"),
        P(None, "tensor"),
        P(),
        P(None, "tensor"),
        P("tensor"),
        P("tensor", "dp"),
    )
    out_specs = (
        P(("dp", "tensor"), None),
        P(("dp", "tensor"), None),
        P(),
        P("dp", "tensor"),
        P("dp", "tensor"),
        P("dp", None),
        P("dp", "tensor"),
        P(None, "tensor"),
        P(),
        P(None, "tensor"),
        P("tensor"),
        P("tensor", "dp"),
    )
    run = functools.partial(body, mesh.shape["dp"], mesh.shape["tensor"])
    return jax.shard_map(run, mesh=mesh, in_specs=in_specs, out_specs=out_specs, check_vma=False)
```

```python
import functools

import jax
import jax.numpy as jnp
from jax import lax
from jax.experimental import pallas as pl
from jax.experimental.pallas import tpu as pltpu
from jax.sharding import PartitionSpec as P

D = 1024
SPAN = 256
SEQLEN = 1024
INNER = 2048
LANES = 128

EPSILON = 1e-05
HIGHEST = lax.Precision.HIGHEST
MESH = pl.DeviceIdType.MESH


def causal(sequence, taps):
    width = taps.shape[0] - 1
    padded = jnp.pad(sequence, ((width - 1, 0), (0, 0)))
    total = jnp.zeros_like(sequence) + taps[width]
    for offset in range(width):
        total = total + taps[offset] * padded[offset : offset + sequence.shape[0]]
    return total


def scan_state(values, step_size, rate, b_map, c_map):
    length, heads, hdim_local = values.shape
    count = length // SPAN
    dots = functools.partial(
        jnp.einsum, precision=lax.Precision.HIGH, preferred_element_type=jnp.float32
    )
    step_c = step_size.reshape(count, SPAN, heads).transpose(0, 2, 1)
    scaled_c = values.reshape(count, SPAN, heads, hdim_local).transpose(0, 2, 1, 3)
    scaled_c = scaled_c * step_c[:, :, :, None]
    b_c = b_map.reshape(count, SPAN, b_map.shape[1])
    c_c = c_map.reshape(count, SPAN, c_map.shape[1])
    lower = (
        lax.broadcasted_iota(jnp.int32, (SPAN, SPAN), 0)
        >= lax.broadcasted_iota(jnp.int32, (SPAN, SPAN), 1)
    )
    logdecay = jnp.einsum(
        "chj,ij->chi", step_c * rate[None, :, None], lower.astype(jnp.float32), precision=HIGHEST
    )
    inner_prod = dots("cin,cjn->cij", c_c, b_c)
    spacing = logdecay[:, :, :, None] - logdecay[:, :, None, :]
    kernel = jnp.where(lower, jnp.exp(jnp.where(lower, spacing, -60.0)), 0.0)
    within = dots("chij,chjp->chip", kernel * inner_prod[:, None], scaled_c)
    last = logdecay[:, :, -1]
    trailing = jnp.exp(last[:, :, None] - logdecay)
    update = dots("chjp,cjn->chpn", scaled_c * trailing[:, :, :, None], b_c)
    fade = jnp.exp(last)
    state = jnp.zeros_like(update[0])
    states = []
    for index in range(count):
        states.append(state)
        state = state * fade[index][:, None, None] + update[index]
    carried = dots("cin,chpn->chip", c_c, jnp.stack(states)) * jnp.exp(logdecay)[:, :, :, None]
    return (within + carried).transpose(0, 2, 1, 3).reshape(length, heads, hdim_local)


def mixer(gate_pre, value_pre, shared_pre, step_pre, conv_value, conv_bc, head_params):
    length = gate_pre.shape[0]
    heads = step_pre.shape[1]
    values = jax.nn.silu(causal(value_pre, conv_value))
    shared = jax.nn.silu(causal(shared_pre, conv_bc))
    half_width = shared.shape[1] // 2
    step_size = jax.nn.softplus(step_pre + head_params[0])
    rate = -jnp.exp(head_params[1])
    headed = values.reshape(length, heads, -1)
    scanned = scan_state(headed, step_size, rate, shared[:, :half_width], shared[:, half_width:])
    scanned = scanned + head_params[2][None, :, None] * headed
    return scanned.reshape(length, -1) * jax.nn.silu(gate_pre)


def contract_rows(left, right):
    return lax.dot_general(
        left, right, (((0,), (0,)), ((), ())), preferred_element_type=jnp.float32
    )


def contract_cols(left, right):
    return lax.dot_general(
        left, right, (((1,), (1,)), ((), ())), preferred_element_type=jnp.float32
    )


def bits_of(size):
    found, bit = [], 1
    while bit < size:
        found.append(bit)
        bit *= 2
    return found


def flip(index, bit):
    return index + bit - 2 * bit * ((index // bit) % 2)


def flip_all(index, mask, bits):
    for bit in bits:
        if mask & bit:
            index = flip(index, bit)
    return index


def reduce_kernel(
    dp, tensor, bc_at, shared_rows, p_ref, small_ref, out_ref, small_out,
    acc, slots, small_slots, bc_send, bc_slots, tsmall_slots,
    send_sem, recv_sem, ssend, srecv, tsend, trecv,
):
    me, rank = lax.axis_index("dp"), lax.axis_index("tensor")
    bits, tbits = bits_of(dp), bits_of(tensor)
    width = p_ref.shape[2]
    cut = (width // LANES + 1) // 2 * LANES
    halves = ((0, cut), (cut, width - cut))
    orders = (bits, bits[:1] + bits[2:] + bits[1:2])
    count = small_ref.shape[0]
    barrier = pltpu.get_barrier_semaphore()
    for bit in bits:
        pl.semaphore_signal(barrier, inc=1, device_id=(flip(me, bit), rank), device_id_type=MESH)
    for bit in tbits:
        pl.semaphore_signal(barrier, inc=1, device_id=(me, flip(rank, bit)), device_id_type=MESH)
    pl.semaphore_wait(barrier, len(bits) + len(tbits))

    slot_of = {}
    sets = []
    for half in range(2):
        order = orders[half]
        seen, number, phases = 0, 0, []
        for phase, bit in enumerate(order):
            seen |= bit
            kept = [r for r in range(dp) if r & seen == 0]
            if phase + 1 < len(order):
                kept.sort(key=lambda r: -(r & order[phase + 1]))
            phases.append(kept)
            for r in kept:
                slot_of[half, phase, r] = number
                number += 1
        sets.append(phases)

    def copy_of(half, phase, r):
        bit = orders[half][phase]
        at, size = halves[half]
        columns = pl.ds(at, size)
        slot = slot_of[half, phase, r]
        if phase == 0:
            source = p_ref.at[flip_all(me, r | bit, bits), :, columns]
        else:
            source = acc.at[r | bit, :, columns]
        return pltpu.make_async_remote_copy(
            src_ref=source,
            dst_ref=slots.at[slot, :, columns],
            send_sem=send_sem.at[half, slot],
            recv_sem=recv_sem.at[half, slot],
            device_id=(flip(me, bit), rank),
            device_id_type=MESH,
        )

    small_out[...] = small_ref[...]
    copies = []

    def small_copy(phase):
        return pltpu.make_async_remote_copy(
            src_ref=small_out,
            dst_ref=small_slots.at[phase],
            send_sem=ssend.at[phase],
            recv_sem=srecv.at[phase],
            device_id=(flip(me, bits[phase]), rank),
            device_id_type=MESH,
        )

    for r_at in range(len(sets[0][0])):
        for half in range(2):
            copy = copy_of(half, 0, sets[half][0][r_at])
            copy.start()
            copies.append(copy)
    for phase in range(len(bits)):
        small = small_copy(phase)
        small.start()
        small.wait()
        small_out[...] += small_slots[phase]
        for r_at in range(len(sets[0][phase])):
            for half in range(2):
                order = orders[half]
                at, size = halves[half]
                columns = pl.ds(at, size)
                r = sets[half][phase][r_at]
                copy_of(half, phase, r).wait_recv()
                arrived = slots[slot_of[half, phase, r], :, columns].astype(jnp.float32)
                if phase == 0:
                    own = p_ref[flip_all(me, r, bits), :, columns]
                else:
                    own = acc[r, :, columns]
                total = own.astype(jnp.float32) + arrived
                if phase + 1 == len(bits):
                    out_ref[:, columns] = total
                else:
                    acc[r, :, columns] = total.astype(jnp.bfloat16)
                    if r & order[phase + 1]:
                        copy = copy_of(half, phase + 1, r ^ order[phase + 1])
                        copy.start()
                        copies.append(copy)
    bc_cols = pl.ds(bc_at, bc_send.shape[1])
    first = count - shared_rows
    for phase, bit in enumerate(tbits):
        bc_send[...] = out_ref[:, bc_cols].astype(jnp.bfloat16)
        pair = []
        for which, (source, target) in enumerate(
            (
                (bc_send, bc_slots.at[phase]),
                (small_out.at[pl.ds(first, shared_rows)], tsmall_slots.at[phase]),
            )
        ):
            copy = pltpu.make_async_remote_copy(
                src_ref=source,
                dst_ref=target,
                send_sem=tsend.at[phase, which],
                recv_sem=trecv.at[phase, which],
                device_id=(me, flip(rank, bit)),
                device_id_type=MESH,
            )
            copy.start()
            pair.append(copy)
        for copy in pair:
            copy.wait()
        out_ref[:, bc_cols] += bc_slots[phase].astype(jnp.float32)
        small_out[pl.ds(first, shared_rows), :] += tsmall_slots[phase]
    for copy in copies:
        copy.wait_send()


def reduce_all(dp, tensor, packed, small, bc_at, bc_width, shared_rows):
    rows, width = packed.shape
    block = rows // dp
    n, t = len(bits_of(dp)), len(bits_of(tensor))
    vmem = pl.BlockSpec(memory_space=pltpu.VMEM)
    return pl.pallas_call(
        functools.partial(reduce_kernel, dp, tensor, bc_at, shared_rows),
        out_shape=(
            jax.ShapeDtypeStruct((block, width), jnp.float32),
            jax.ShapeDtypeStruct(small.shape, jnp.float32),
        ),
        in_specs=[vmem, vmem],
        out_specs=(vmem, vmem),
        scratch_shapes=[
            pltpu.VMEM((dp, block, width), jnp.bfloat16),
            pltpu.VMEM((dp - 1, block, width), jnp.bfloat16),
            pltpu.VMEM((n,) + small.shape, jnp.float32),
            pltpu.VMEM((block, bc_width), jnp.bfloat16),
            pltpu.VMEM((t, block, bc_width), jnp.bfloat16),
            pltpu.VMEM((t, shared_rows, LANES), jnp.float32),
            pltpu.SemaphoreType.DMA((2, dp - 1)),
            pltpu.SemaphoreType.DMA((2, dp - 1)),
            pltpu.SemaphoreType.DMA((n,)),
            pltpu.SemaphoreType.DMA((n,)),
            pltpu.SemaphoreType.DMA((t, 2)),
            pltpu.SemaphoreType.DMA((t, 2)),
        ],
        compiler_params=pltpu.CompilerParams(
            collective_id=0, has_side_effects=True, vmem_limit_bytes=48 * 1024 * 1024
        ),
    )(packed.reshape(dp, block, width), small)


def as_rows(parts, rows):
    flat = jnp.concatenate([part.reshape(-1) for part in parts])
    return jnp.pad(flat, (0, rows * LANES - flat.shape[0])).reshape(rows, LANES)


def body(
    dp,
    tensor,
    tokens,
    cotangent,
    norm_gain,
    w_gate,
    w_value,
    w_bc,
    w_step,
    conv_value,
    conv_bc,
    head_params,
    gnorm_gain,
    w_out,
):
    width, bc_width, heads = w_gate.shape[1], w_bc.shape[1], w_step.shape[1]
    rows32 = tokens.astype(jnp.float32)
    grad_out = cotangent.astype(jnp.float32)
    scaling = lax.rsqrt(jnp.mean(rows32 * rows32, axis=1, keepdims=True) + EPSILON)
    normed = lax.all_gather(
        (rows32 * scaling * norm_gain).astype(jnp.bfloat16), "tensor", axis=0, tiled=True
    )
    shard = jnp.concatenate(
        [w_gate, w_value, w_bc, jnp.pad(w_step, ((0, 0), (0, LANES - heads))), w_out.T], axis=1
    )
    fetched = lax.all_gather(shard, "dp", axis=0, tiled=True)
    grad_rows = lax.all_gather(cotangent, "tensor", axis=0, tiled=True)
    at = 2 * width + bc_width + LANES
    w_cat, w_out_t = fetched[:, :at], fetched[:, at:]
    projected = jnp.dot(normed, w_cat, preferred_element_type=jnp.float32)
    pieces = (
        projected[:, :width],
        projected[:, width : 2 * width],
        projected[:, 2 * width : 2 * width + bc_width],
        projected[:, 2 * width + bc_width : 2 * width + bc_width + heads],
    )
    gated, mix_back = jax.vjp(mixer, *pieces, conv_value, conv_bc, head_params)
    grad_scaled = jnp.dot(grad_rows, w_out_t, preferred_element_type=jnp.float32)
    grad_unit = grad_scaled * gnorm_gain
    sums = lax.psum(
        jnp.stack([jnp.sum(gated * gated, axis=1), jnp.sum(grad_unit * gated, axis=1)]), "tensor"
    )
    rescale = lax.rsqrt(sums[0] / INNER + EPSILON)[:, None]
    unitized = gated * rescale
    scaled = (unitized * gnorm_gain).astype(jnp.bfloat16)
    branch = contract_cols(scaled, w_out_t)
    block_out = rows32 + lax.psum_scatter(
        branch.astype(jnp.bfloat16), "tensor", scatter_dimension=0, tiled=True
    ).astype(jnp.float32)
    grad_w_out_t = contract_rows(grad_rows, scaled)
    grad_gnorm = jnp.sum(grad_scaled * unitized, axis=0)
    grad_gated = (
        rescale * grad_unit - gated * (rescale * rescale * rescale) * sums[1][:, None] / INNER
    )
    mix_grads = mix_back(grad_gated)
    grad_cat = jnp.concatenate(
        [piece.astype(jnp.bfloat16) for piece in mix_grads[:3]]
        + [jnp.pad(mix_grads[3].astype(jnp.bfloat16), ((0, 0), (0, LANES - heads)))],
        axis=1,
    )
    grad_conv_value, grad_conv_bc, grad_head = mix_grads[4:]
    grad_normed = contract_cols(grad_cat, w_cat)
    grad_h = lax.psum_scatter(
        grad_normed.astype(jnp.bfloat16), "tensor", scatter_dimension=0, tiled=True
    ).astype(jnp.float32)
    scaled_grad = grad_h * norm_gain
    grad_input = (
        grad_out
        + scaling * scaled_grad
        - rows32
        * (scaling * scaling * scaling)
        * jnp.sum(scaled_grad * rows32, axis=1, keepdims=True)
        / D
    )
    grad_norm_local = jnp.sum(grad_h * rows32 * scaling, axis=0)
    weight_terms = jnp.concatenate([contract_rows(normed, grad_cat), grad_w_out_t], axis=1)
    own_parts = [grad_conv_value, grad_gnorm, jnp.pad(grad_head, ((0, 0), (0, LANES - heads)))]
    own_rows = -(-(sum(part.size for part in own_parts)) // (8 * LANES)) * 8
    shared_parts = [grad_conv_bc, grad_norm_local]
    shared_rows = -(-(sum(part.size for part in shared_parts)) // (8 * LANES)) * 8
    small = jnp.concatenate([as_rows(own_parts, own_rows), as_rows(shared_parts, shared_rows)])
    summed, small = reduce_all(
        dp, tensor, weight_terms.astype(jnp.bfloat16), small, 2 * width, bc_width, shared_rows
    )
    own, shared = small[:own_rows].reshape(-1), small[own_rows:].reshape(-1)
    n_conv, n_bc = grad_conv_value.size, grad_conv_bc.size
    return (
        block_out,
        grad_input,
        shared[n_bc : n_bc + norm_gain.shape[0]],
        summed[:, :width],
        summed[:, width : 2 * width],
        summed[:, 2 * width : 2 * width + bc_width],
        summed[:, 2 * width + bc_width : 2 * width + bc_width + heads],
        own[:n_conv].reshape(grad_conv_value.shape),
        shared[:n_bc].reshape(grad_conv_bc.shape),
        own[n_conv + width : n_conv + width + 3 * LANES].reshape(3, LANES)[:, :heads],
        own[n_conv : n_conv + width],
        summed[:, at:].T,
    )


def solution(mesh):
    in_specs = (
        P(("dp", "tensor"), None),
        P(("dp", "tensor"), None),
        P(),
        P("dp", "tensor"),
        P("dp", "tensor"),
        P("dp", None),
        P("dp", "tensor"),
        P(None, "tensor"),
        P(),
        P(None, "tensor"),
        P("tensor"),
        P("tensor", "dp"),
    )
    out_specs = (
        P(("dp", "tensor"), None),
        P(("dp", "tensor"), None),
        P(),
        P("dp", "tensor"),
        P("dp", "tensor"),
        P("dp", None),
        P("dp", "tensor"),
        P(None, "tensor"),
        P(),
        P(None, "tensor"),
        P("tensor"),
        P("tensor", "dp"),
    )
    run = functools.partial(body, mesh.shape["dp"], mesh.shape["tensor"])
    return jax.shard_map(run, mesh=mesh, in_specs=in_specs, out_specs=out_specs, check_vma=False)
```
